128 devices in a mesh: row: 16 (over z, x_hi, core), col: 8 (over x_lo, y).
Axes of the slice: x: 4 (x_hi: 2, x_lo: 2; x = x_hi * 2 + x_lo), y: 4, z: 4, core: 2. Of those that a mesh axis runs over, the one named last changes fastest.
Arguments:
- spectra: bfloat16 [16, 1024, 2, 1024], P('row', None, None, 'col'), may hold values from -6 to 6
Outputs:
- correlations: bfloat16 [1024, 1024, 512], P('row', 'col')
The draws below stay inside these ranges and needn't reach their ends.
All inputs are finite; a program needn't handle non-finite values.
Results may differ from the reference program's by a relative error of at most 0.0068.
Values may be sent and summed in bfloat16 or wider, within the bound.
No kernel may reach another device: no remote copies, remote signals or barrier semaphores. Data moves between devices by JAX's collectives and lax.ppermute only.
A program may use at most 256 MiB of HBM per device.

```python
import math
import jax
import jax.numpy as jnp
from jax import lax

C = 1024
F = 1024
L = 512
K = 8
W = 16


def level_of(rng, shape, pieces, low, largest):
    factor_of = 1.0
    for dim, blocks in pieces:
        draws = jax.random.uniform(jax.random.fold_in(jax.random.fold_in(rng, 6), dim), (blocks,), jnp.float32, low / len(pieces), largest / len(pieces))
        factor_of = factor_of * jnp.repeat(jnp.exp(draws), shape[dim] // blocks).reshape((-1,) + (1,) * (len(shape) - 1 - dim))
    return factor_of


def gaussian(own_key, dims, scale, reach, cuts=(), held_as=jnp.bfloat16):
    loudness = level_of(own_key, dims, cuts, -0.22, 0.18) if cuts else 1.0
    values = jax.random.normal(own_key, dims, jnp.float32) * scale * loudness
    return jnp.minimum(jnp.maximum(values, -reach), reach).astype(held_as)


def setup_inputs(seed: int = 0) -> dict:
    streams_of = jax.random.split(jax.random.key(seed), 2)
    spectra = gaussian(streams_of[0], (W, C, 2, F), 1.0, 6.0, ((0, 16), (3, 8)))
    return {"spectra": spectra}


def lag_tables(freqs):
    lags = jnp.arange(L, dtype=jnp.int32) - L // 2
    phase = freqs[:, None] * lags[None, :] % (2 * F)
    angle = phase.astype(jnp.float32) * (math.pi / F)
    return (jnp.cos(angle).astype(jnp.bfloat16), jnp.sin(angle).astype(jnp.bfloat16))

def whiten(spectra):
    values = spectra.astype(jnp.float32)
    magnitude = jnp.sqrt(values[:, :, 0] ** 2 + values[:, :, 1] ** 2)
    padded = jnp.pad(magnitude, ((0, 0), (0, 0), (K, K)))
    total = jnp.zeros_like(magnitude)
    for offset_bin in range(2 * K + 1):
        total = total + padded[:, :, offset_bin:offset_bin + F]
    smooth = jnp.maximum(total / (2 * K + 1), 0.5)
    return (values / smooth[:, :, None, :]).astype(jnp.bfloat16)

def reference(spectra):
    white = whiten(spectra)
    cos_table, sin_table = lag_tables(jnp.arange(F, dtype=jnp.int32))
    rblock = math.gcd(C, 64)
    col_re = white[:, :, 0].astype(jnp.float32)
    col_im = white[:, :, 1].astype(jnp.float32)
    scale = 1.0 / math.sqrt(W * F)

    def one_block(index):
        first_row = index * rblock
        row_re = lax.dynamic_slice_in_dim(col_re, first_row, rblock, 1)
        row_im = lax.dynamic_slice_in_dim(col_im, first_row, rblock, 1)
        real_part = (jnp.einsum('wif,wjf->ijf', row_re, col_re) + jnp.einsum('wif,wjf->ijf', row_im, col_im)).astype(jnp.bfloat16)
        imag_part = (jnp.einsum('wif,wjf->ijf', row_re, col_im) - jnp.einsum('wif,wjf->ijf', row_im, col_re)).astype(jnp.bfloat16)
        lagged = jnp.dot(real_part.reshape(rblock * C, F), cos_table, preferred_element_type=jnp.float32)
        lagged = lagged - jnp.dot(imag_part.reshape(rblock * C, F), sin_table, preferred_element_type=jnp.float32)
        lagged = lagged.reshape(rblock, C, L) * scale
        rows_global = first_row + jnp.arange(rblock, dtype=jnp.int32)
        same = rows_global[:, None] == jnp.arange(C, dtype=jnp.int32)[None, :]
        return jnp.where(same[:, :, None], jnp.float32(0.0), lagged).astype(jnp.bfloat16)
    blocks = lax.map(one_block, jnp.arange(C // rblock, dtype=jnp.int32))
    return blocks.reshape(C, C, L)
```

```python
import functools
import math

import jax
import jax.numpy as jnp
import numpy as np
from jax import lax
from jax.experimental import pallas as pl
from jax.experimental.pallas import tpu as pltpu
from jax.sharding import PartitionSpec as P

F = 1024
L = 512
K = 8
W = 16
BF = jnp.bfloat16
F32 = jnp.float32

ROWS, COLS = 16, 8
Z_UP = [(r, (r + 4) % 16) for r in range(16)]
Z_DOWN = [(r, (r - 4) % 16) for r in range(16)]
SIBLING = [(r, r ^ 1) for r in range(16)]
Y_UP = [(c, (c & 4) | ((c + 1) & 3)) for c in range(8)]
Y_DOWN = [(c, (c & 4) | ((c - 1) & 3)) for c in range(8)]
GROUPS_R = [
    [(z * 4 + xh * 2 + k) * 8 + c for xh in range(2) for c in range(8)]
    for z in range(4)
    for k in range(2)
]
GROUPS_L = [[r * 8 + xl * 4 + y for xl in range(2) for r in range(16)] for y in range(4)]
STEP_I = 4


def tables():
    freqs = np.arange(F)
    t_cos = np.concatenate([np.arange(257), np.zeros(15, np.int64)])
    t_sin = np.arange(256)
    t_sin[0] = 256
    cos = np.cos((t_cos[:, None] * freqs % (2 * F)) * (math.pi / F))
    sin = np.sin((t_sin[:, None] * freqs % (2 * F)) * (math.pi / F))
    cos[257:] = 0.0

    def by_block(table):
        blocks = table.reshape(table.shape[0], 2, 4, 128)
        return blocks.transpose(2, 0, 1, 3).reshape(4, table.shape[0], 256)

    flip = np.zeros((256, 256))
    flip[0, 0] = 1.0
    for k in range(1, 256):
        flip[k, 256 - k] = 1.0
    return [jnp.asarray(a, BF) for a in (by_block(cos), by_block(sin), flip)]


def band():
    rows = np.arange(128)[:, None]
    taps = np.arange(144)[None, :]
    return ((taps >= rows) & (taps <= rows + 2 * K)).astype(np.float32)


def whiten_kernel(x_ref, before_ref, after_ref, band_ref, right_ref, left_ref):
    re = x_ref[:, 0:128].astype(F32).T
    im = x_ref[:, 128:256].astype(F32).T

    def magnitude(a, b):
        return jnp.sqrt(a * a + b * b)

    before = before_ref[...].astype(F32)
    after = after_ref[...].astype(F32)
    extended = jnp.concatenate(
        [magnitude(before[0:8], before[8:16]), magnitude(re, im), magnitude(after[0:8], after[8:16])], axis=0
    )
    total = jnp.dot(band_ref[...], extended, precision=lax.Precision.HIGHEST, preferred_element_type=F32)
    smooth = jnp.maximum(total / (2 * K + 1), 0.5)
    re = re / smooth
    im = im / smooth
    for g in range(16):
        both = jnp.concatenate([re[8 * g : 8 * g + 8], im[8 * g : 8 * g + 8]], axis=0).astype(BF)
        for c in range(COLS):
            right_ref[c, g] = both[:, 128 * c : 128 * c + 128]
    left_ref[:, 0:128] = re.T.astype(BF)
    left_ref[:, 128:256] = im.T.astype(BF)


def whiten(x, before, after):
    return pl.pallas_call(
        whiten_kernel,
        out_shape=(
            jax.ShapeDtypeStruct((COLS, 16, 16, 128), BF),
            jax.ShapeDtypeStruct((1024, 256), BF),
        ),
        compiler_params=pltpu.CompilerParams(vmem_limit_bytes=40 << 20),
        name="whiten",
    )(x, before, after, jnp.asarray(band()))


def regroup_kernel(order_ref, in_ref, out_ref):
    granule = lax.broadcasted_iota(jnp.int32, (64, 128), 1) // 8
    for block in range(2):
        for half in range(2):
            rows = []
            for slot in range(8):
                window = order_ref[half * 8 + slot]
                for p in range(2):
                    rows.append(in_ref[block * 16 + window, :, 128 * p : 128 * p + 128].astype(F32))
            for bit in (1, 2, 4, 8):
                low = (granule & bit) == 0
                new = list(rows)
                for u in range(16):
                    if u & bit:
                        continue
                    a, b = rows[u], rows[u | bit]
                    new[u] = jnp.where(low, a, pltpu.roll(b, 8 * bit, 1))
                    new[u | bit] = jnp.where(low, pltpu.roll(a, 128 - 8 * bit, 1), b)
                rows = new
            for g in range(16):
                out_ref[block, :, g * 256 + half * 128 : g * 256 + half * 128 + 128] = rows[g].astype(BF)


def regroup(pieces, order):
    return pl.pallas_call(
        regroup_kernel,
        out_shape=jax.ShapeDtypeStruct((2, 64, 4096), BF),
        in_specs=[pl.BlockSpec(memory_space=pltpu.SMEM), pl.BlockSpec(memory_space=pltpu.VMEM)],
        out_specs=pl.BlockSpec(memory_space=pltpu.VMEM),
        compiler_params=pltpu.CompilerParams(vmem_limit_bytes=40 << 20),
        name="regroup",
    )(order, pieces)


def correlate_kernel(halved, first, last, place_ref, *refs):
    chunks = len(halved)
    refs = list(refs)
    lefts, rights, coss, sins = [], [], [], []
    for is_halved in halved:
        lefts.append([refs.pop(0) for _ in range(2 if is_halved else 1)])
        rights.append([refs.pop(0) for _ in range(10)])
        coss.append(refs.pop(0))
        sins.append(refs.pop(0))
    flip_ref = refs.pop(0)
    before_ref = None if first else refs.pop(0)
    out_ref, x_ref = refs

    step = pl.program_id(0)

    @pl.when(step == 0)
    def cross():
        row = lax.broadcasted_iota(jnp.int32, (8, 256), 0)
        lane = lax.broadcasted_iota(jnp.int32, (8, 256), 1)
        mask = jnp.where((lane % 8) == row, 1.0, 0.0).astype(F32)[None]
        for n in range(chunks):
            for block in range(2):

                def one(g, n, block):
                    at = pl.multiple_of(g * 256, 256)
                    if halved[n]:
                        left = lefts[n][block][:, pl.ds(at, 256)]
                    else:
                        left = lefts[n][0][block, :, pl.ds(at, 256)]
                    left = (left.astype(F32)[:, None, :] * mask).astype(BF).reshape(512, 256)
                    tiles = []
                    for side in range(2):
                        own, up, down, far_a, far_b = rights[n][5 * side : 5 * side + 5]
                        for ref in (own, up, down):
                            for w in range(2):
                                tiles.append(ref[w, block, 0, g])
                        far = (far_a, far_b)[block]
                        for w in range(2):
                            tiles.append(far[w, 0, g])
                    swapped = []
                    for tile in tiles:
                        wide = tile.astype(F32)
                        swapped.append(jnp.concatenate([wide[8:16], -wide[0:8]], axis=0).astype(BF))
                    right = jnp.concatenate(
                        [jnp.concatenate(tiles, axis=0), jnp.concatenate(swapped, axis=0)], axis=1
                    )
                    return jnp.dot(left, right, preferred_element_type=F32).reshape(64, 8, 256)

                def pair(h, carry, n=n, block=block):
                    both = jnp.concatenate([one(2 * h, n, block), one(2 * h + 1, n, block)], axis=1)
                    both = both.astype(BF).reshape(32, 2, 16, 256)
                    at = pl.ds(pl.multiple_of(n * 256 + block * 128 + h * 16, 16), 16)
                    for q in range(2):
                        for odd in range(2):
                            x_ref[q, :, at, 128 * odd : 128 * odd + 128] = both[
                                :, odd, :, 128 * q : 128 * q + 128
                            ]
                    return carry

                lax.fori_loop(0, 8, pair, 0)

    lane = lax.broadcasted_iota(jnp.int32, (1, 256), 1)
    top = lax.broadcasted_iota(jnp.int32, (256, 256), 0) == 0
    for u in range(STEP_I // 2):
        at = step * (STEP_I // 2) + u
        even = jnp.zeros((272, 256), F32)
        odd = jnp.zeros((256, 256), F32)
        for n in range(chunks):
            even = even + jnp.dot(
                coss[n][0], x_ref[0, at, 256 * n : 256 * n + 256], preferred_element_type=F32
            )
            odd = odd + jnp.dot(
                sins[n][0], x_ref[1, at, 256 * n : 256 * n + 256], preferred_element_type=F32
            )
        if not first:
            even = even + before_ref[u, 0:272]
            odd = odd + before_ref[u, 272:528]
        if not last:
            out_ref[u, 0:272] = even
            out_ref[u, 272:528] = odd
            continue
        row_global = place_ref[4] * 64 + at * 2 + lane // 128
        col_global = place_ref[5] * 128 + lane % 128
        factor = jnp.where(row_global == col_global, 0.0, 1.0 / math.sqrt(W * F)).astype(F32)
        even = even * factor
        odd = odd * factor
        later = even[0:256] - jnp.where(top, 0.0, odd)
        earlier = jnp.where(top, even[256:257], even[0:256]) + odd
        earlier = jnp.dot(flip_ref[...], earlier.astype(BF), preferred_element_type=F32)
        for half in range(2):
            cols = slice(128 * half, 128 * half + 128)
            out_ref[2 * u + half, :, 0:256] = earlier[:, cols].T.astype(BF)
            out_ref[2 * u + half, :, 256:512] = later[:, cols].T.astype(BF)


def correlate(place, chunk_list, before, last, tabs):
    cos, sin, flip = tabs
    steps = 64 // STEP_I
    halved = tuple(len(lefts) == 2 for _, lefts, _ in chunk_list)
    args, specs = [], []
    for slot, lefts, rights in chunk_list:
        for a in lefts:
            args.append(a)
            specs.append(pl.BlockSpec(a.shape, lambda s, p, n=a.ndim: (0,) * n))
        for a in rights:
            if a.shape[1] == 128:
                args.append(a.reshape(2, 2, 4, 16, 16, 128))
                specs.append(
                    pl.BlockSpec((2, 2, 1, 16, 16, 128), lambda s, p, k=slot: (0, 0, p[k], 0, 0, 0))
                )
            else:
                args.append(a.reshape(2, 4, 16, 16, 128))
                specs.append(pl.BlockSpec((2, 1, 16, 16, 128), lambda s, p, k=slot: (0, p[k], 0, 0, 0)))
        args += [cos, sin]
        specs.append(pl.BlockSpec((1, 272, 256), lambda s, p, k=slot: (p[k], 0, 0)))
        specs.append(pl.BlockSpec((1, 256, 256), lambda s, p, k=slot: (p[k], 0, 0)))
    args.append(flip)
    specs.append(pl.BlockSpec((256, 256), lambda s, p: (0, 0)))
    held = pl.BlockSpec((STEP_I // 2, 528, 256), lambda s, p: (s, 0, 0))
    if before is not None:
        args.append(before)
        specs.append(held)
    if last:
        out_shape = jax.ShapeDtypeStruct((64, 128, L), BF)
        out_spec = pl.BlockSpec((STEP_I, 128, L), lambda s, p: (s, 0, 0))
    else:
        out_shape = jax.ShapeDtypeStruct((32, 528, 256), F32)
        out_spec = held
    n = len(chunk_list)
    return pl.pallas_call(
        functools.partial(correlate_kernel, halved, before is None, last),
        out_shape=out_shape,
        grid_spec=pltpu.PrefetchScalarGridSpec(
            num_scalar_prefetch=1,
            grid=(steps,),
            in_specs=specs,
            out_specs=out_spec,
            scratch_shapes=[pltpu.VMEM((2, 32, 256 * n, 256), BF)],
        ),
        compiler_params=pltpu.CompilerParams(vmem_limit_bytes=60 << 20),
        cost_estimate=pl.CostEstimate(
            flops=n * 4_400_000_000, bytes_accessed=n * 3 * 2**20 + 2**24, transcendentals=0
        ),
        name="correlate",
    )(place, *args)


def body(spectra):
    row = lax.axis_index("row")
    col = lax.axis_index("col")
    x = spectra.reshape(1024, 256)
    edges = spectra[0].transpose(1, 2, 0)
    last_bins = edges[:, 120:128].reshape(16, 1024)
    first_bins = edges[:, 0:8].reshape(16, 1024)
    before = lax.ppermute(last_bins, "col", [(i, i + 1) for i in range(COLS - 1)])
    after = lax.ppermute(first_bins, "col", [(i + 1, i) for i in range(COLS - 1)])
    right, left = whiten(x, before, after)

    right = lax.all_to_all(
        jnp.concatenate([right, right], axis=0), ("row", "col"), split_axis=0, concat_axis=0, tiled=True,
        axis_index_groups=GROUPS_R,
    )
    right = right.reshape(2, 128, 16, 128)
    up = lax.ppermute(right, "row", Z_UP)
    down = lax.ppermute(right, "row", Z_DOWN)
    left = left.reshape(16, 64, 256)
    left = lax.all_to_all(
        jnp.concatenate([left, left], axis=0), ("row", "col"), split_axis=0, concat_axis=0, tiled=True,
        axis_index_groups=GROUPS_L,
    )
    far_a = lax.ppermute(up[:, 0:64], "row", Z_UP)
    far_b = lax.ppermute(down[:, 64:128], "row", Z_DOWN)

    z, core = row // 4, row % 2
    slots = jnp.arange(16, dtype=jnp.int32)
    shift = jnp.array([0, 0, 3, 3, 1, 1, 2, 2] * 2, jnp.int32)
    order = ((z + shift) % 4) * 4 + (slots % 2) * 2 + (core + slots // 8) % 2
    left = regroup(left, order)
    left_up = lax.ppermute(left, "col", Y_UP)
    left_down = lax.ppermute(left, "col", Y_DOWN)
    mine = [right, up, down, far_a, far_b]
    theirs = [lax.ppermute(a, "row", SIBLING) for a in mine]
    rights = mine + theirs
    left_far_a = lax.ppermute(left_up[0], "col", Y_UP)
    left_far_b = lax.ppermute(left_down[1], "col", Y_DOWN)

    y = col % 4
    place = jnp.stack([y, (y + 3) % 4, (y + 1) % 4, (y + 2) % 4, row, col]).astype(jnp.int32)
    tabs = tables()
    held = correlate(place, [(0, [left], rights)], None, False, tabs)
    held = correlate(place, [(1, [left_up], rights), (2, [left_down], rights)], held, False, tabs)
    return correlate(place, [(3, [left_far_a, left_far_b], rights)], held, True, tabs)


def solution(mesh):
    return jax.shard_map(
        body,
        mesh=mesh,
        in_specs=(P("row", None, None, "col"),),
        out_specs=P("row", "col", None),
        check_vma=False,
    )
```

```python
import functools
import math

import jax
import jax.numpy as jnp
import numpy as np
from jax import lax
from jax.experimental import pallas as pl
from jax.experimental.pallas import tpu as pltpu
from jax.sharding import PartitionSpec as P

F = 1024
L = 512
K = 8
W = 16
BF = jnp.bfloat16
F32 = jnp.float32

ROWS, COLS = 16, 8
SIBLING = [(r, r ^ 1) for r in range(16)]
Z_APART = [(r, (r + (4 if r % 2 == 0 else -4)) % 16) for r in range(16)]
Y_UP = [(c, (c & 4) | ((c + 1) & 3)) for c in range(8)]
Y_DOWN = [(c, (c & 4) | ((c - 1) & 3)) for c in range(8)]
GROUPS_R = [
    [(z * 4 + xh * 2 + k) * 8 + c for xh in range(2) for c in range(8)]
    for z in range(4)
    for k in range(2)
]
GROUPS_L = [[r * 8 + xl * 4 + y for xl in range(2) for r in range(16)] for y in range(4)]
HELD = 0
GROUP = 4
STEP_I = 16


def tables():
    freqs = np.arange(F)
    t_cos = np.concatenate([np.arange(257), np.zeros(15, np.int64)])
    t_sin = np.arange(256)
    t_sin[0] = 256
    cos = np.cos((t_cos[:, None] * freqs % (2 * F)) * (math.pi / F))
    sin = np.sin((t_sin[:, None] * freqs % (2 * F)) * (math.pi / F))
    cos[257:] = 0.0

    def by_block(table):
        blocks = table.reshape(table.shape[0], 2, 4, 128)
        return blocks.transpose(2, 0, 1, 3).reshape(4, table.shape[0], 256)

    return [jnp.asarray(a, BF) for a in (by_block(cos), by_block(sin))]


def band():
    rows = np.arange(128)[:, None]
    taps = np.arange(144)[None, :]
    return ((taps >= rows) & (taps <= rows + 2 * K)).astype(np.float32)


def turn_kernel(x_ref, right_ref, first_ref, last_ref):
    re = x_ref[:, 0:128].astype(F32).T
    im = x_ref[:, 128:256].astype(F32).T
    for g in range(16):
        both = jnp.concatenate([re[8 * g : 8 * g + 8], im[8 * g : 8 * g + 8]], axis=0).astype(BF)
        for c in range(COLS):
            right_ref[c, g] = both[:, 128 * c : 128 * c + 128]
            right_ref[COLS + c, g] = both[:, 128 * c : 128 * c + 128]
        if g == 0:
            first_ref[...] = both
        if g == 15:
            last_ref[...] = both


def turn(x):
    return pl.pallas_call(
        turn_kernel,
        out_shape=(
            jax.ShapeDtypeStruct((2 * COLS, 16, 16, 128), BF),
            jax.ShapeDtypeStruct((16, 1024), BF),
            jax.ShapeDtypeStruct((16, 1024), BF),
        ),
        compiler_params=pltpu.CompilerParams(vmem_limit_bytes=40 << 20),
        name="turn",
    )(x)


def magnitude(a, b):
    return jnp.sqrt(a * a + b * b)


def whiten_left_kernel(x_ref, before_ref, after_ref, band_ref, left_ref):
    re = x_ref[:, 0:128].astype(F32).T
    im = x_ref[:, 128:256].astype(F32).T
    before = before_ref[...].astype(F32)
    after = after_ref[...].astype(F32)
    extended = jnp.concatenate(
        [magnitude(before[0:8], before[8:16]), magnitude(re, im), magnitude(after[0:8], after[8:16])], axis=0
    )
    total = jnp.dot(band_ref[...], extended, precision=lax.Precision.HIGHEST, preferred_element_type=F32)
    smooth = jnp.maximum(total / (2 * K + 1), 0.5)
    re = (re / smooth).T.astype(BF)
    im = (im / smooth).T.astype(BF)
    for copy in range(2):
        for r in range(ROWS):
            left_ref[copy * ROWS + r, :, 0:128] = re[64 * r : 64 * r + 64]
            left_ref[copy * ROWS + r, :, 128:256] = im[64 * r : 64 * r + 64]


def whiten_left(x, before, after):
    return pl.pallas_call(
        whiten_left_kernel,
        out_shape=jax.ShapeDtypeStruct((2 * ROWS, 64, 256), BF),
        compiler_params=pltpu.CompilerParams(vmem_limit_bytes=40 << 20),
        name="whiten_left",
    )(x, before, after, jnp.asarray(band()))


def whiten_right_kernel(place_ref, x_ref, band_ref, after_ref, out_ref, re_ref, im_ref, ext_ref):
    del after_ref
    re_ref[...] = x_ref[:, :, 0:8].astype(F32)
    im_ref[...] = x_ref[:, :, 8:16].astype(F32)
    for w in range(2):
        ext_ref[0:8, 128 * w : 128 * w + 128] = jnp.zeros((8, 128), F32)
        ext_ref[1032:1040, 128 * w : 128 * w + 128] = jnp.zeros((8, 128), F32)
        ext_ref[8:1032, 128 * w : 128 * w + 128] = magnitude(re_ref[w], im_ref[w]).reshape(1024, 128)
    for block in range(8):
        wide = ext_ref[128 * block : 128 * block + 144]
        high = wide.astype(BF)
        rest = wide - high.astype(F32)
        middle = rest.astype(BF)
        low = (rest - middle.astype(F32)).astype(BF)
        total = jnp.dot(
            band_ref[...], jnp.concatenate([high, middle, low], axis=0), preferred_element_type=F32
        )
        smooth = jnp.maximum(total / (2 * K + 1), 0.5)
        for w in range(2):
            here = smooth[:, 128 * w : 128 * w + 128].reshape(16, 8, 128)
            rows = slice(16 * block, 16 * block + 16)
            re_ref[w, rows] = re_ref[w, rows] / here
            im_ref[w, rows] = im_ref[w, rows] / here
    for n in range(4):
        for half in range(2):
            rows = pl.ds((place_ref[n] + 4 * half) * 16, 16)
            for w in range(2):
                both = jnp.concatenate([re_ref[w, rows], im_ref[w, rows]], axis=1).astype(BF)
                out_ref[n, w, half] = both


def whiten_right(raw, place, after):
    bands = np.concatenate([band()] * 3, axis=1)
    return pl.pallas_call(
        whiten_right_kernel,
        out_shape=jax.ShapeDtypeStruct((4, 2, 2, 16, 16, 128), BF),
        in_specs=[
            pl.BlockSpec(memory_space=pltpu.SMEM),
            pl.BlockSpec(memory_space=pltpu.VMEM),
            pl.BlockSpec(memory_space=pltpu.VMEM),
            pl.BlockSpec(memory_space=pl.ANY),
        ],
        out_specs=pl.BlockSpec(memory_space=pltpu.VMEM),
        scratch_shapes=[
            pltpu.VMEM((2, 128, 8, 128), F32),
            pltpu.VMEM((2, 128, 8, 128), F32),
            pltpu.VMEM((1040, 256), F32),
        ],
        compiler_params=pltpu.CompilerParams(vmem_limit_bytes=40 << 20),
        name="whiten_right",
    )(place, raw, jnp.asarray(bands, BF), after)


def regroup_kernel(order_ref, in_ref, out_ref):
    granule = lax.broadcasted_iota(jnp.int32, (64, 128), 1) // 8
    for block in range(2):
        for half in range(2):
            rows = []
            for slot in range(8):
                window = order_ref[half * 8 + slot]
                for p in range(2):
                    rows.append(in_ref[block * 16 + window, :, 128 * p : 128 * p + 128].astype(F32))
            for bit in (1, 2, 4, 8):
                low = (granule & bit) == 0
                new = list(rows)
                for u in range(16):
                    if u & bit:
                        continue
                    a, b = rows[u], rows[u | bit]
                    new[u] = jnp.where(low, a, pltpu.roll(b, 8 * bit, 1))
                    new[u | bit] = jnp.where(low, pltpu.roll(a, 128 - 8 * bit, 1), b)
                rows = new
            for g in range(16):
                at = g * 256 + half * 128
                out_ref[block, :, at : at + 128] = rows[g].astype(BF)


def regroup(pieces, order):
    return pl.pallas_call(
        regroup_kernel,
        out_shape=jax.ShapeDtypeStruct((2, 64, 4096), BF),
        in_specs=[pl.BlockSpec(memory_space=pltpu.SMEM), pl.BlockSpec(memory_space=pltpu.VMEM)],
        out_specs=pl.BlockSpec(memory_space=pltpu.VMEM),
        compiler_params=pltpu.CompilerParams(vmem_limit_bytes=40 << 20),
        name="regroup",
    )(order, pieces)


def bin_mask():
    row = lax.broadcasted_iota(jnp.int32, (8, 256), 0)
    lane = lax.broadcasted_iota(jnp.int32, (8, 256), 1)
    return jnp.where((lane % 8) == row, 1.0, 0.0).astype(F32)[None]


def cross_bins(left, tiles, mask):
    left = (left.astype(F32)[:, None, :] * mask).astype(BF).reshape(512, 256)
    swapped = []
    for tile in tiles:
        wide = tile.astype(F32)
        swapped.append(jnp.concatenate([wide[8:16], -wide[0:8]], axis=0).astype(BF))
    right = jnp.concatenate([jnp.concatenate(tiles, axis=0), jnp.concatenate(swapped, axis=0)], axis=1)
    return jnp.dot(left, right, preferred_element_type=F32).reshape(64, 8, 256)


def store_bins(x_ref, at, first, second):
    both = jnp.concatenate([first, second], axis=1).astype(BF).reshape(64 // GROUP, GROUP, 16, 256)
    for q in range(2):
        for i in range(GROUP):
            x_ref[q, :, pl.ds(at, 16), 128 * i : 128 * i + 128] = both[:, i, :, 128 * q : 128 * q + 128]


def cross_kernel(place_ref, left_a_ref, left_b_ref, *refs):
    del place_ref
    rights, (out_ref, x_ref, left_ref, left_sems, sems) = refs[:8], refs[8:]
    loads = [
        pltpu.make_async_copy(ref, left_ref.at[half], left_sems.at[half])
        for half, ref in enumerate((left_a_ref, left_b_ref))
    ]
    for load in loads:
        load.start()
    for load in loads:
        load.wait()
    mask = bin_mask()

    def send(part):
        bins = pl.ds(pl.multiple_of(part * 64, 64), 64)
        return pltpu.make_async_copy(x_ref.at[:, :, bins, :], out_ref.at[:, :, bins, :], sems.at[part])

    def quarter(part, carry):
        block, first = part // 2, 8 * (part % 2)

        def one(g):
            tiles = [ref[w, block, g] for ref in rights for w in range(2)]
            at = pl.multiple_of(g * 256, 256)
            return cross_bins(left_ref[block, :, pl.ds(at, 256)], tiles, mask)

        for h in range(4):
            at = pl.multiple_of(part * 64 + 16 * h, 16)
            store_bins(x_ref, at, one(first + 2 * h), one(first + 2 * h + 1))
        send(part).start()
        return carry

    lax.fori_loop(0, 4, quarter, 0)
    for part in range(4):
        send(part).wait()


def cross(place, lefts, rights, chunk):
    specs = [pl.BlockSpec(memory_space=pl.ANY)] * 2
    specs += [pl.BlockSpec((None, 2, 2, 16, 16, 128), lambda s, p: (p[6 + chunk], 0, 0, 0, 0, 0))] * 8
    return pl.pallas_call(
        cross_kernel,
        out_shape=jax.ShapeDtypeStruct((2, 64 // GROUP, 256, 128 * GROUP), BF),
        grid_spec=pltpu.PrefetchScalarGridSpec(
            num_scalar_prefetch=1,
            grid=(1,),
            in_specs=specs,
            out_specs=pl.BlockSpec(memory_space=pl.ANY),
            scratch_shapes=[
                pltpu.VMEM((2, 64 // GROUP, 256, 128 * GROUP), BF),
                pltpu.VMEM((2, 64, 4096), BF),
                pltpu.SemaphoreType.DMA((2,)),
                pltpu.SemaphoreType.DMA((4,)),
            ],
        ),
        compiler_params=pltpu.CompilerParams(vmem_limit_bytes=48 << 20),
        cost_estimate=pl.CostEstimate(flops=5_000_000_000, bytes_accessed=12 * 2**20, transcendentals=0),
        name="cross",
    )(place, *lefts, *rights)


def lags_kernel(held, fresh, place_ref, cos_ref, sin_ref, *refs):
    refs = list(refs)
    lefts = [refs.pop(0) for _ in range(fresh + 1)]
    rights = [refs.pop(0) for _ in range(8)]
    xs = [refs.pop(0) for _ in range(held)]
    out_ref, x_ref, left_ref, right_ref, result_ref, x_sems, left_sems, right_sems, out_sems = refs

    def load_x(n):
        return pltpu.make_async_copy(xs[n], x_ref.at[n], x_sems.at[n])

    def load_left(n, half):
        source = lefts[n].at[half] if n < fresh - 1 else lefts[n + half]
        return pltpu.make_async_copy(source, left_ref.at[n, half], left_sems.at[n, half])

    def load_right(n, a):
        return pltpu.make_async_copy(
            rights[a].at[place_ref[6 + held + n]], right_ref.at[n, a], right_sems.at[n, a]
        )

    for n in range(fresh):
        for half in range(2):
            load_left(n, half).start()
        for a in range(8):
            load_right(n, a).start()
    for n in range(held):
        load_x(n).start()
    mask = bin_mask()
    for n in range(fresh):
        for half in range(2):
            load_left(n, half).wait()
        for a in range(8):
            load_right(n, a).wait()

    def quarter(index, carry):
        n, part = index // 4, index % 4
        block, first = part // 2, 8 * (part % 2)

        def one(g):
            at = pl.multiple_of(g * 256, 256)
            tiles = [right_ref[n, a, w, block, g] for a in range(8) for w in range(2)]
            return cross_bins(left_ref[n, block, :, pl.ds(at, 256)], tiles, mask)

        for h in range(4):
            at = pl.multiple_of(part * 64 + 16 * h, 16)
            store_bins(x_ref.at[held + n], at, one(first + 2 * h), one(first + 2 * h + 1))
        return carry

    lax.fori_loop(0, 4 * fresh, quarter, 0)
    for n in range(held):
        load_x(n).wait()

    width = 128 * GROUP
    lane = lax.broadcasted_iota(jnp.int32, (1, width), 1)
    top = lax.broadcasted_iota(jnp.int32, (256, width), 0) == 0
    column = lax.broadcasted_iota(jnp.int32, (128, 128), 1)
    mirror = (128 - column) % 128

    def send(s, slot):
        return pltpu.make_async_copy(
            result_ref.at[slot], out_ref.at[pl.ds(s * STEP_I, STEP_I)], out_sems.at[slot]
        )

    def step(s, carry):
        slot = lax.rem(s, 2)

        @pl.when(s >= 2)
        def free():
            send(s - 2, slot).wait()

        for u in range(STEP_I // GROUP):
            at = s * (STEP_I // GROUP) + u
            even = odd = None
            for n in range(4):
                part = jnp.dot(cos_ref[place_ref[n]], x_ref[n, 0, at], preferred_element_type=F32)
                even = part if even is None else even + part
            for n in range(4):
                part = jnp.dot(sin_ref[place_ref[n]], x_ref[n, 1, at], preferred_element_type=F32)
                odd = part if odd is None else odd + part
            row_global = place_ref[4] * 64 + at * GROUP + lane // 128
            col_global = place_ref[5] * 128 + lane % 128
            factor = jnp.where(row_global == col_global, 0.0, 1.0 / math.sqrt(W * F)).astype(F32)
            even = even * factor
            odd = odd * factor
            later = even[0:256] - jnp.where(top, 0.0, odd)
            earlier = jnp.where(top, even[256:257], even[0:256]) + odd
            for i in range(GROUP):
                cols = slice(128 * i, 128 * i + 128)
                near = jnp.take_along_axis(earlier[0:128, cols].T, mirror, axis=1, mode="promise_in_bounds")
                away = jnp.take_along_axis(earlier[128:256, cols].T, mirror, axis=1, mode="promise_in_bounds")
                here = GROUP * u + i
                result_ref[slot, here, :, 0:128] = jnp.where(column == 0, near, away).astype(BF)
                result_ref[slot, here, :, 128:256] = jnp.where(column == 0, away, near).astype(BF)
                result_ref[slot, here, :, 256:512] = later[:, cols].T.astype(BF)
        send(s, slot).start()
        return carry

    steps = 64 // STEP_I
    lax.fori_loop(0, steps, step, 0)
    for s in range(steps - 2, steps):
        send(s, s % 2).wait()


def lags(place, lefts, rights, xs, tabs):
    cos, sin = tabs
    held, fresh = len(xs), len(lefts) - 1
    whole = pl.BlockSpec(memory_space=pltpu.VMEM)
    remote = pl.BlockSpec(memory_space=pl.ANY)
    return pl.pallas_call(
        functools.partial(lags_kernel, held, fresh),
        out_shape=jax.ShapeDtypeStruct((64, 128, L), BF),
        in_specs=[pl.BlockSpec(memory_space=pltpu.SMEM), whole, whole] + [remote] * (fresh + 1 + 8 + held),
        out_specs=remote,
        scratch_shapes=[
            pltpu.VMEM((4, 2, 64 // GROUP, 256, 128 * GROUP), BF),
            pltpu.VMEM((fresh, 2, 64, 4096), BF),
            pltpu.VMEM((fresh, 8, 2, 2, 16, 16, 128), BF),
            pltpu.VMEM((2, STEP_I, 128, L), BF),
            pltpu.SemaphoreType.DMA((max(held, 1),)),
            pltpu.SemaphoreType.DMA((fresh, 2)),
            pltpu.SemaphoreType.DMA((fresh, 8)),
            pltpu.SemaphoreType.DMA((2,)),
        ],
        compiler_params=pltpu.CompilerParams(vmem_limit_bytes=60 << 20),
        cost_estimate=pl.CostEstimate(flops=18_000_000_000, bytes_accessed=36 * 2**20, transcendentals=0),
        name="lags",
    )(place, cos, sin, *lefts, *rights, *xs)


def marker_kernel(*refs):
    refs[-1][...] = jnp.zeros((8, 128), F32)


def marker(cost, *after):
    return pl.pallas_call(
        marker_kernel,
        out_shape=jax.ShapeDtypeStruct((8, 128), F32),
        in_specs=[pl.BlockSpec(memory_space=pl.ANY)] * len(after),
        out_specs=pl.BlockSpec(memory_space=pltpu.VMEM),
        cost_estimate=pl.CostEstimate(flops=cost * 10**9, bytes_accessed=0, transcendentals=0),
        name="marker",
    )(*after)


def body(spectra):
    row = lax.axis_index("row")
    col = lax.axis_index("col")
    z, core = row // 4, row % 2
    y = col % 4
    near = jnp.where(core == 0, 3, 1)
    far = 4 - near
    blocks = jnp.stack([y, (y + 3) % 4, (y + 1) % 4, (y + 2) % 4])
    place = jnp.concatenate([blocks, jnp.stack([row, col]), jnp.arange(4)]).astype(jnp.int32)
    blocks = blocks.astype(jnp.int32)

    x = spectra.reshape(1024, 256)
    raw, first, last = turn(x)
    raw = lax.all_to_all(
        raw, ("row", "col"), split_axis=0, concat_axis=0, tiled=True, axis_index_groups=GROUPS_R
    )
    before = lax.ppermute(last, "col", [(i, i + 1) for i in range(COLS - 1)])
    after = lax.ppermute(first, "col", [(i + 1, i) for i in range(COLS - 1)])
    white = whiten_left(x, before, after)
    left = lax.all_to_all(
        white, ("row", "col"), split_axis=0, concat_axis=0, tiled=True, axis_index_groups=GROUPS_L
    )
    right = whiten_right(raw.reshape(2, 128, 16, 128), blocks, white)

    shift = jnp.stack([0 * z, 0 * z, near, near, 2 + 0 * z, far, far, 2 + 0 * z])
    swap = jnp.array([0, 1, 0, 1, 0, 1, 0, 1], jnp.int32)
    order = (((z + shift) % 4) * 4 + (core + swap) % 2)[:, None] + jnp.array([[0, 2]], jnp.int32)

    right_later, left = lax.optimization_barrier((right, left))
    sibling = lax.ppermute(right_later, "row", SIBLING)
    near_a = lax.ppermute(right_later, "row", Z_APART)
    near_b = lax.ppermute(sibling, "row", Z_APART)
    left = regroup(left, order.reshape(16).astype(jnp.int32))
    up = lax.ppermute(left, "col", Y_UP)
    down = lax.ppermute(left, "col", Y_DOWN)
    token = marker(100, left, sibling)

    near_a, token = lax.optimization_barrier((near_a, token))
    far_a = lax.ppermute(near_a, "row", Z_APART)
    swapped_a = lax.ppermute(near_a, "row", SIBLING)
    token = marker(100, token)

    up, down, near_b, token = lax.optimization_barrier((up, down, near_b, token))
    far_first = lax.ppermute(up[0], "col", Y_UP)
    far_second = lax.ppermute(down[1], "col", Y_DOWN)
    swapped_b = lax.ppermute(near_b, "row", SIBLING)
    token = marker(100, token)

    far_a, far_first, far_second, token = lax.optimization_barrier((far_a, far_first, far_second, token))
    swapped_far = lax.ppermute(far_a, "row", SIBLING)
    rights = [right, sibling, near_a, near_b, far_a, swapped_a, swapped_b, swapped_far]
    lefts = [left, up, down, far_first, far_second]
    return lags(place, lefts, rights, [], tables())


def solution(mesh):
    return jax.shard_map(
        body,
        mesh=mesh,
        in_specs=(P("row", None, None, "col"),),
        out_specs=P("row", "col", None),
        check_vma=False,
    )
```

```python
import functools
import math

import jax
import jax.numpy as jnp
import numpy as np
from jax import lax
from jax.experimental import pallas as pl
from jax.experimental.pallas import tpu as pltpu
from jax.sharding import PartitionSpec as P

F = 1024
L = 512
K = 8
W = 16
BF = jnp.bfloat16
F32 = jnp.float32

ROWS, COLS = 16, 8
SIBLING = [(r, r ^ 1) for r in range(16)]
Z_APART = [(r, (r + (4 if r % 2 == 0 else -4)) % 16) for r in range(16)]
Y_APART = [
    (r * 8 + c, r * 8 + ((c & 4) | ((c + (1 if r % 2 == 0 else -1)) & 3))) for r in range(16) for c in range(8)
]
Y_AGAINST = [(there, here) for here, there in Y_APART]
GROUPS_R = [
    [(z * 4 + xh * 2 + k) * 8 + c for xh in range(2) for c in range(8)]
    for z in range(4)
    for k in range(2)
]
GROUPS_L = [[r * 8 + xl * 4 + y for xl in range(2) for r in range(16)] for y in range(4)]
GROUP = 2
STEP_I = 16


def tables():
    freqs = np.arange(F)
    t_cos = np.concatenate([np.arange(257), np.zeros(15, np.int64)])
    t_sin = np.arange(256)
    t_sin[0] = 256
    cos = np.cos((t_cos[:, None] * freqs % (2 * F)) * (math.pi / F))
    sin = np.sin((t_sin[:, None] * freqs % (2 * F)) * (math.pi / F))
    cos[257:] = 0.0

    def by_block(table):
        blocks = table.reshape(table.shape[0], 2, 4, 128)
        return blocks.transpose(2, 0, 1, 3).reshape(4, table.shape[0], 256)

    return [jnp.asarray(a, BF) for a in (by_block(cos), by_block(sin))]


def band():
    rows = np.arange(128)[:, None]
    taps = np.arange(144)[None, :]
    return ((taps >= rows) & (taps <= rows + 2 * K)).astype(np.float32)


def turn_kernel(x_ref, right_ref, first_ref, last_ref):
    re = x_ref[:, 0:128].astype(F32).T
    im = x_ref[:, 128:256].astype(F32).T
    for g in range(16):
        both = jnp.concatenate([re[8 * g : 8 * g + 8], im[8 * g : 8 * g + 8]], axis=0).astype(BF)
        for c in range(COLS):
            right_ref[c, g] = both[:, 128 * c : 128 * c + 128]
            right_ref[COLS + c, g] = both[:, 128 * c : 128 * c + 128]
        if g == 0:
            first_ref[...] = both
        if g == 15:
            last_ref[...] = both


def turn(x):
    return pl.pallas_call(
        turn_kernel,
        out_shape=(
            jax.ShapeDtypeStruct((2 * COLS, 16, 16, 128), BF),
            jax.ShapeDtypeStruct((16, 1024), BF),
            jax.ShapeDtypeStruct((16, 1024), BF),
        ),
        compiler_params=pltpu.CompilerParams(vmem_limit_bytes=40 << 20),
        name="turn",
    )(x)


def magnitude(a, b):
    return jnp.sqrt(a * a + b * b)


def whiten_left_kernel(x_ref, before_ref, after_ref, band_ref, left_ref):
    re = x_ref[:, 0:128].astype(F32).T
    im = x_ref[:, 128:256].astype(F32).T
    before = before_ref[...].astype(F32)
    after = after_ref[...].astype(F32)
    extended = jnp.concatenate(
        [magnitude(before[0:8], before[8:16]), magnitude(re, im), magnitude(after[0:8], after[8:16])], axis=0
    )
    total = jnp.dot(band_ref[...], extended, precision=lax.Precision.HIGHEST, preferred_element_type=F32)
    smooth = jnp.maximum(total / (2 * K + 1), 0.5)
    re = (re / smooth).T.astype(BF)
    im = (im / smooth).T.astype(BF)
    for copy in range(2):
        for r in range(ROWS):
            left_ref[copy * ROWS + r, :, 0:128] = re[64 * r : 64 * r + 64]
            left_ref[copy * ROWS + r, :, 128:256] = im[64 * r : 64 * r + 64]


def whiten_left(x, before, after):
    return pl.pallas_call(
        whiten_left_kernel,
        out_shape=jax.ShapeDtypeStruct((2 * ROWS, 64, 256), BF),
        compiler_params=pltpu.CompilerParams(vmem_limit_bytes=40 << 20),
        name="whiten_left",
    )(x, before, after, jnp.asarray(band()))


def whiten_right_kernel(place_ref, x_ref, band_ref, after_ref, out_ref, re_ref, im_ref, ext_ref):
    del after_ref
    re_ref[...] = x_ref[:, :, 0:8].astype(F32)
    im_ref[...] = x_ref[:, :, 8:16].astype(F32)
    for w in range(2):
        ext_ref[0:8, 128 * w : 128 * w + 128] = jnp.zeros((8, 128), F32)
        ext_ref[1032:1040, 128 * w : 128 * w + 128] = jnp.zeros((8, 128), F32)
        ext_ref[8:1032, 128 * w : 128 * w + 128] = magnitude(re_ref[w], im_ref[w]).reshape(1024, 128)
    for block in range(8):
        wide = ext_ref[128 * block : 128 * block + 144]
        high = wide.astype(BF)
        rest = wide - high.astype(F32)
        middle = rest.astype(BF)
        low = (rest - middle.astype(F32)).astype(BF)
        total = jnp.dot(
            band_ref[...], jnp.concatenate([high, middle, low], axis=0), preferred_element_type=F32
        )
        smooth = jnp.maximum(total / (2 * K + 1), 0.5)
        for w in range(2):
            here = smooth[:, 128 * w : 128 * w + 128].reshape(16, 8, 128)
            rows = slice(16 * block, 16 * block + 16)
            re_ref[w, rows] = re_ref[w, rows] / here
            im_ref[w, rows] = im_ref[w, rows] / here
    for n in range(4):
        for half in range(2):
            rows = pl.ds((place_ref[n] + 4 * half) * 16, 16)
            for w in range(2):
                both = jnp.concatenate([re_ref[w, rows], im_ref[w, rows]], axis=1).astype(BF)
                out_ref[n, w, half] = both


def whiten_right(raw, place, after):
    bands = np.concatenate([band()] * 3, axis=1)
    return pl.pallas_call(
        whiten_right_kernel,
        out_shape=jax.ShapeDtypeStruct((4, 2, 2, 16, 16, 128), BF),
        in_specs=[
            pl.BlockSpec(memory_space=pltpu.SMEM),
            pl.BlockSpec(memory_space=pltpu.VMEM),
            pl.BlockSpec(memory_space=pltpu.VMEM),
            pl.BlockSpec(memory_space=pl.ANY),
        ],
        out_specs=pl.BlockSpec(memory_space=pltpu.VMEM),
        scratch_shapes=[
            pltpu.VMEM((2, 128, 8, 128), F32),
            pltpu.VMEM((2, 128, 8, 128), F32),
            pltpu.VMEM((1040, 256), F32),
        ],
        compiler_params=pltpu.CompilerParams(vmem_limit_bytes=40 << 20),
        name="whiten_right",
    )(place, raw, jnp.asarray(bands, BF), after)


def regroup_kernel(order_ref, in_ref, out_ref):
    granule = lax.broadcasted_iota(jnp.int32, (64, 128), 1) // 8
    for block in range(2):
        for half in range(2):
            rows = []
            for slot in range(8):
                window = order_ref[half * 8 + slot]
                for p in range(2):
                    rows.append(in_ref[block * 16 + window, :, 128 * p : 128 * p + 128].astype(F32))
            for bit in (1, 2, 4, 8):
                low = (granule & bit) == 0
                new = list(rows)
                for u in range(16):
                    if u & bit:
                        continue
                    a, b = rows[u], rows[u | bit]
                    new[u] = jnp.where(low, a, pltpu.roll(b, 8 * bit, 1))
                    new[u | bit] = jnp.where(low, pltpu.roll(a, 128 - 8 * bit, 1), b)
                rows = new
            for g in range(16):
                at = g * 256 + half * 128
                out_ref[block, :, at : at + 128] = rows[g].astype(BF)


def regroup(pieces, order):
    return pl.pallas_call(
        regroup_kernel,
        out_shape=jax.ShapeDtypeStruct((2, 64, 4096), BF),
        in_specs=[pl.BlockSpec(memory_space=pltpu.SMEM), pl.BlockSpec(memory_space=pltpu.VMEM)],
        out_specs=pl.BlockSpec(memory_space=pltpu.VMEM),
        compiler_params=pltpu.CompilerParams(vmem_limit_bytes=40 << 20),
        cost_estimate=pl.CostEstimate(flops=2 * 10**9, bytes_accessed=0, transcendentals=0),
        name="regroup",
    )(order, pieces)


def bin_mask():
    row = lax.broadcasted_iota(jnp.int32, (8, 256), 0)
    lane = lax.broadcasted_iota(jnp.int32, (8, 256), 1)
    return (lane % 8 == row)[None]


def cross_bins(left, tiles, mask):
    left = jnp.where(mask, jnp.broadcast_to(left.astype(F32)[:, None, :], (64, 8, 256)), 0.0)
    left = left.astype(BF).reshape(512, 256)
    swapped = []
    for tile in tiles:
        wide = tile.astype(F32)
        swapped.append(jnp.concatenate([wide[8:16], -wide[0:8]], axis=0).astype(BF))
    right = jnp.concatenate([jnp.concatenate(tiles, axis=0), jnp.concatenate(swapped, axis=0)], axis=1)
    return jnp.dot(left, right, preferred_element_type=F32).reshape(64, 8, 256)


def store_bins(x_ref, at, first, second):
    both = jnp.concatenate([first, second], axis=1).astype(BF).reshape(64 // GROUP, GROUP, 16, 256)
    for q in range(2):
        for i in range(GROUP):
            x_ref[q, :, pl.ds(at, 16), 128 * i : 128 * i + 128] = both[:, i, :, 128 * q : 128 * q + 128]


def lags_kernel(held, fresh, place_ref, cos_ref, sin_ref, *refs):
    refs = list(refs)
    lefts = [refs.pop(0) for _ in range(fresh)]
    rights = [refs.pop(0) for _ in range(8)]
    xs = [refs.pop(0) for _ in range(held)]
    out_ref, x_ref, left_ref, right_ref, result_ref, x_sems, left_sems, right_sems, out_sems = refs

    def load_x(n):
        return pltpu.make_async_copy(xs[n], x_ref.at[n], x_sems.at[n])

    def load_left(n):
        return pltpu.make_async_copy(lefts[n], left_ref.at[n], left_sems.at[n])

    def load_right(n, a):
        return pltpu.make_async_copy(
            rights[a].at[place_ref[6 + held + n]], right_ref.at[n, a], right_sems.at[n, a]
        )

    for n in range(fresh):
        load_left(n).start()
        for a in range(8):
            load_right(n, a).start()
    for n in range(held):
        load_x(n).start()
    mask = bin_mask()
    def quarter(index, carry):
        n, part = index // 4, index % 4
        block, first = part // 2, 8 * (part % 2)

        @pl.when(part == 0)
        def arrived():
            pltpu.make_async_copy(lefts[0], left_ref.at[n], left_sems.at[n]).wait()
            for a in range(8):
                pltpu.make_async_copy(rights[a].at[0], right_ref.at[n, a], right_sems.at[n, a]).wait()

        def one(g):
            at = pl.multiple_of(g * 256, 256)
            tiles = [right_ref[n, a, w, block, g] for a in range(8) for w in range(2)]
            return cross_bins(left_ref[n, block, :, pl.ds(at, 256)], tiles, mask)

        for h in range(4):
            at = pl.multiple_of(part * 64 + 16 * h, 16)
            store_bins(x_ref.at[held + n], at, one(first + 2 * h), one(first + 2 * h + 1))
        return carry

    lax.fori_loop(0, 4 * fresh, quarter, 0)
    for n in range(held):
        load_x(n).wait()

    width = 128 * GROUP
    lane = lax.broadcasted_iota(jnp.int32, (1, width), 1)
    top = lax.broadcasted_iota(jnp.int32, (256, width), 0) == 0
    column = lax.broadcasted_iota(jnp.int32, (128, 128), 1)
    mirror = (128 - column) % 128

    def send(s, slot):
        return pltpu.make_async_copy(
            result_ref.at[slot], out_ref.at[pl.ds(s * STEP_I, STEP_I)], out_sems.at[slot]
        )

    def step(s, carry):
        slot = lax.rem(s, 2)

        @pl.when(s >= 2)
        def free():
            send(s - 2, slot).wait()

        for u in range(STEP_I // GROUP):
            at = s * (STEP_I // GROUP) + u
            even = odd = None
            for n in range(4):
                part = jnp.dot(cos_ref[place_ref[n]], x_ref[n, 0, at], preferred_element_type=F32)
                even = part if even is None else even + part
            for n in range(4):
                part = jnp.dot(sin_ref[place_ref[n]], x_ref[n, 1, at], preferred_element_type=F32)
                odd = part if odd is None else odd + part
            row_global = place_ref[4] * 64 + at * GROUP + lane // 128
            col_global = place_ref[5] * 128 + lane % 128
            factor = jnp.where(row_global == col_global, 0.0, 1.0 / math.sqrt(W * F)).astype(F32)
            even = even * factor
            odd = odd * factor
            later = even[0:256] - jnp.where(top, 0.0, odd)
            earlier = jnp.where(top, even[256:257], even[0:256]) + odd
            for i in range(GROUP):
                cols = slice(128 * i, 128 * i + 128)
                near = jnp.take_along_axis(earlier[0:128, cols].T, mirror, axis=1, mode="promise_in_bounds")
                away = jnp.take_along_axis(earlier[128:256, cols].T, mirror, axis=1, mode="promise_in_bounds")
                here = GROUP * u + i
                result_ref[slot, here, :, 0:128] = jnp.where(column == 0, near, away).astype(BF)
                result_ref[slot, here, :, 128:256] = jnp.where(column == 0, away, near).astype(BF)
                result_ref[slot, here, :, 256:512] = later[:, cols].T.astype(BF)
        send(s, slot).start()
        return carry

    steps = 64 // STEP_I
    lax.fori_loop(0, steps, step, 0)
    for s in range(steps - 2, steps):
        send(s, s % 2).wait()


def lags(place, lefts, rights, xs, tabs):
    cos, sin = tabs
    held, fresh = len(xs), len(lefts)
    whole = pl.BlockSpec(memory_space=pltpu.VMEM)
    remote = pl.BlockSpec(memory_space=pl.ANY)
    return pl.pallas_call(
        functools.partial(lags_kernel, held, fresh),
        out_shape=jax.ShapeDtypeStruct((64, 128, L), BF),
        in_specs=[pl.BlockSpec(memory_space=pltpu.SMEM), whole, whole] + [remote] * (fresh + 8 + held),
        out_specs=remote,
        scratch_shapes=[
            pltpu.VMEM((4, 2, 64 // GROUP, 256, 128 * GROUP), BF),
            pltpu.VMEM((fresh, 2, 64, 4096), BF),
            pltpu.VMEM((fresh, 8, 2, 2, 16, 16, 128), BF),
            pltpu.VMEM((2, STEP_I, 128, L), BF),
            pltpu.SemaphoreType.DMA((max(held, 1),)),
            pltpu.SemaphoreType.DMA((fresh,)),
            pltpu.SemaphoreType.DMA((fresh, 8)),
            pltpu.SemaphoreType.DMA((2,)),
        ],
        compiler_params=pltpu.CompilerParams(vmem_limit_bytes=60 << 20),
        cost_estimate=pl.CostEstimate(flops=18_000_000_000, bytes_accessed=36 * 2**20, transcendentals=0),
        name="lags",
    )(place, cos, sin, *lefts, *rights, *xs)


def marker_kernel(*refs):
    refs[-1][...] = jnp.zeros((8, 128), F32)


def marker(*after):
    return pl.pallas_call(
        marker_kernel,
        out_shape=jax.ShapeDtypeStruct((8, 128), F32),
        in_specs=[pl.BlockSpec(memory_space=pl.ANY)] * len(after),
        out_specs=pl.BlockSpec(memory_space=pltpu.VMEM),
        cost_estimate=pl.CostEstimate(flops=100_000_000_000, bytes_accessed=0, transcendentals=0),
        name="marker",
    )(*after)


def body(spectra):
    row = lax.axis_index("row")
    col = lax.axis_index("col")
    z, core = row // 4, row % 2
    y = col % 4
    near = jnp.where(core == 0, 3, 1)
    far = 4 - near
    place = jnp.stack(
        [y, (y + near) % 4, (y + far) % 4, (y + 2) % 4, row, col, 0 * y, 1 + core, 2 - core, 3 + 0 * y]
    ).astype(jnp.int32)
    blocks = jnp.stack([y, (y + 3) % 4, (y + 1) % 4, (y + 2) % 4]).astype(jnp.int32)

    both = ("row", "col")
    x = spectra.reshape(1024, 256)
    raw, first, last = turn(x)
    raw = lax.all_to_all(
        raw, ("row", "col"), split_axis=0, concat_axis=0, tiled=True, axis_index_groups=GROUPS_R
    )
    before = lax.ppermute(last, "col", [(i, i + 1) for i in range(COLS - 1)])
    after = lax.ppermute(first, "col", [(i + 1, i) for i in range(COLS - 1)])
    white = whiten_left(x, before, after)
    left = lax.all_to_all(
        white, ("row", "col"), split_axis=0, concat_axis=0, tiled=True, axis_index_groups=GROUPS_L
    )
    right = whiten_right(raw.reshape(2, 128, 16, 128), blocks, white)

    shift = jnp.stack([0 * z, 0 * z, near, near, 2 + 0 * z, far, far, 2 + 0 * z])
    swap = jnp.array([0, 1, 0, 1, 0, 1, 0, 1], jnp.int32)
    order = (((z + shift) % 4) * 4 + (core + swap) % 2)[:, None] + jnp.array([[0, 2]], jnp.int32)
    wait = lax.optimization_barrier
    right_later, left = wait((right, left))
    near_a = lax.ppermute(right_later, "row", Z_APART)
    sibling = lax.ppermute(right_later, "row", SIBLING)
    left = regroup(left, order.reshape(16).astype(jnp.int32))
    left_near = lax.ppermute(left, both, Y_APART)
    left_other = lax.ppermute(left, both, Y_AGAINST)
    near_b = lax.ppermute(sibling, "row", Z_APART)
    token = marker(left, sibling)

    left_near, near_a, token = wait((left_near, near_a, token))
    left_far = lax.ppermute(left_near, both, Y_APART)
    far_a = lax.ppermute(near_a, "row", Z_APART)
    token = marker(token)

    left_other, near_b, token = wait((left_other, near_b, token))
    swapped = [lax.ppermute(a, "row", SIBLING) for a in (near_a, near_b)]
    token = marker(token)
    left_far, far_a, token = wait((left_far, far_a, token))
    swapped.append(lax.ppermute(far_a, "row", SIBLING))
    token = marker(token)
    place, _ = wait((place, token))
    rights = [right, sibling, near_a, near_b, far_a] + swapped
    return lags(place, [left, left_near, left_other, left_far], rights, [], tables())


def solution(mesh):
    return jax.shard_map(
        body,
        mesh=mesh,
        in_specs=(P("row", None, None, "col"),),
        out_specs=P("row", "col", None),
        check_vma=False,
    )
```

```python
import functools
import math

import jax
import jax.numpy as jnp
import numpy as np
from jax import lax
from jax.experimental import pallas as pl
from jax.experimental.pallas import tpu as pltpu
from jax.sharding import PartitionSpec as P

F = 1024
L = 512
K = 8
W = 16
BF = jnp.bfloat16
F32 = jnp.float32

ROWS, COLS = 16, 8
SIBLING = [(r, r ^ 1) for r in range(16)]
Z_APART = [(r, (r + (4 if r % 2 == 0 else -4)) % 16) for r in range(16)]
Y_APART = [
    (r * 8 + c, r * 8 + ((c & 4) | ((c + (1 if r % 2 == 0 else -1)) & 3))) for r in range(16) for c in range(8)
]
Y_AGAINST = [(there, here) for here, there in Y_APART]
GROUPS_R = [
    [(z * 4 + xh * 2 + k) * 8 + c for xh in range(2) for c in range(8)]
    for z in range(4)
    for k in range(2)
]
GROUPS_L = [[r * 8 + xl * 4 + y for xl in range(2) for r in range(16)] for y in range(4)]
GROUP = 2
STEP_I = 16


def tables():
    freqs = np.arange(F)
    t_cos = np.concatenate([np.arange(257), np.zeros(15, np.int64)])
    t_sin = np.arange(256)
    t_sin[0] = 256
    cos = np.cos((t_cos[:, None] * freqs % (2 * F)) * (math.pi / F))
    sin = np.sin((t_sin[:, None] * freqs % (2 * F)) * (math.pi / F))
    cos[257:] = 0.0

    def by_block(table):
        blocks = table.reshape(table.shape[0], 2, 4, 128)
        return blocks.transpose(2, 0, 1, 3).reshape(4, table.shape[0], 256)

    return [jnp.asarray(a, BF) for a in (by_block(cos), by_block(sin))]


def band(copies):
    row = lax.broadcasted_iota(jnp.int32, (128, 144 * copies), 0)
    tap = lax.broadcasted_iota(jnp.int32, (128, 144 * copies), 1) % 144
    return jnp.where((tap >= row) & (tap <= row + 2 * K), 1.0, 0.0).astype(F32)


def turn_kernel(x_ref, right_ref, first_ref, last_ref):
    re = x_ref[:, 0:128].astype(F32).T
    im = x_ref[:, 128:256].astype(F32).T
    for g in range(16):
        both = jnp.concatenate([re[8 * g : 8 * g + 8], im[8 * g : 8 * g + 8]], axis=0).astype(BF)
        for c in range(COLS):
            right_ref[c, g] = both[:, 128 * c : 128 * c + 128]
            right_ref[COLS + c, g] = both[:, 128 * c : 128 * c + 128]
        if g == 0:
            first_ref[...] = both
        if g == 15:
            last_ref[...] = both


def turn(x):
    return pl.pallas_call(
        turn_kernel,
        out_shape=(
            jax.ShapeDtypeStruct((2 * COLS, 16, 16, 128), BF),
            jax.ShapeDtypeStruct((16, 1024), BF),
            jax.ShapeDtypeStruct((16, 1024), BF),
        ),
        compiler_params=pltpu.CompilerParams(vmem_limit_bytes=40 << 20),
        name="turn",
    )(x)


def magnitude(a, b):
    return jnp.sqrt(a * a + b * b)


def whiten_left_kernel(x_ref, before_ref, after_ref, left_ref):
    re = x_ref[:, 0:128].astype(F32).T
    im = x_ref[:, 128:256].astype(F32).T
    before = before_ref[...].astype(F32)
    after = after_ref[...].astype(F32)
    extended = jnp.concatenate(
        [magnitude(before[0:8], before[8:16]), magnitude(re, im), magnitude(after[0:8], after[8:16])], axis=0
    )
    total = jnp.dot(band(1), extended, precision=lax.Precision.HIGHEST, preferred_element_type=F32)
    smooth = jnp.maximum(total / (2 * K + 1), 0.5)
    re = (re / smooth).T.astype(BF)
    im = (im / smooth).T.astype(BF)
    for copy in range(2):
        for r in range(ROWS):
            left_ref[copy * ROWS + r, :, 0:128] = re[64 * r : 64 * r + 64]
            left_ref[copy * ROWS + r, :, 128:256] = im[64 * r : 64 * r + 64]


def whiten_left(x, before, after):
    return pl.pallas_call(
        whiten_left_kernel,
        out_shape=jax.ShapeDtypeStruct((2 * ROWS, 64, 256), BF),
        compiler_params=pltpu.CompilerParams(vmem_limit_bytes=40 << 20),
        name="whiten_left",
    )(x, before, after)


def whiten_right_kernel(place_ref, x_ref, after_ref, out_ref, re_ref, im_ref, ext_ref):
    del after_ref
    re_ref[...] = x_ref[:, :, 0:8].astype(F32)
    im_ref[...] = x_ref[:, :, 8:16].astype(F32)
    for w in range(2):
        ext_ref[0:8, 128 * w : 128 * w + 128] = jnp.zeros((8, 128), F32)
        ext_ref[1032:1040, 128 * w : 128 * w + 128] = jnp.zeros((8, 128), F32)
        ext_ref[8:1032, 128 * w : 128 * w + 128] = magnitude(re_ref[w], im_ref[w]).reshape(1024, 128)
    bands = band(3).astype(BF)
    for block in range(8):
        wide = ext_ref[128 * block : 128 * block + 144]
        high = wide.astype(BF)
        rest = wide - high.astype(F32)
        middle = rest.astype(BF)
        low = (rest - middle.astype(F32)).astype(BF)
        total = jnp.dot(
            bands, jnp.concatenate([high, middle, low], axis=0), preferred_element_type=F32
        )
        smooth = jnp.maximum(total / (2 * K + 1), 0.5)
        for w in range(2):
            here = smooth[:, 128 * w : 128 * w + 128].reshape(16, 8, 128)
            rows = slice(16 * block, 16 * block + 16)
            re_ref[w, rows] = re_ref[w, rows] / here
            im_ref[w, rows] = im_ref[w, rows] / here
    for n in range(4):
        for half in range(2):
            rows = pl.ds((place_ref[n] + 4 * half) * 16, 16)
            for w in range(2):
                both = jnp.concatenate([re_ref[w, rows], im_ref[w, rows]], axis=1).astype(BF)
                out_ref[n, w, half] = both


def whiten_right(raw, place, after):
    return pl.pallas_call(
        whiten_right_kernel,
        out_shape=jax.ShapeDtypeStruct((4, 2, 2, 16, 16, 128), BF),
        in_specs=[
            pl.BlockSpec(memory_space=pltpu.SMEM),
            pl.BlockSpec(memory_space=pltpu.VMEM),
            pl.BlockSpec(memory_space=pl.ANY),
        ],
        out_specs=pl.BlockSpec(memory_space=pltpu.VMEM),
        scratch_shapes=[
            pltpu.VMEM((2, 128, 8, 128), F32),
            pltpu.VMEM((2, 128, 8, 128), F32),
            pltpu.VMEM((1040, 256), F32),
        ],
        compiler_params=pltpu.CompilerParams(vmem_limit_bytes=40 << 20),
        name="whiten_right",
    )(place, raw, after)


def regroup_kernel(order_ref, in_ref, out_ref):
    granule = lax.broadcasted_iota(jnp.int32, (64, 128), 1) // 8
    for block in range(2):
        for half in range(2):
            rows = []
            for slot in range(8):
                window = order_ref[half * 8 + slot]
                for p in range(2):
                    rows.append(in_ref[block * 16 + window, :, 128 * p : 128 * p + 128].astype(F32))
            for bit in (1, 2, 4, 8):
                low = (granule & bit) == 0
                new = list(rows)
                for u in range(16):
                    if u & bit:
                        continue
                    a, b = rows[u], rows[u | bit]
                    new[u] = jnp.where(low, a, pltpu.roll(b, 8 * bit, 1))
                    new[u | bit] = jnp.where(low, pltpu.roll(a, 128 - 8 * bit, 1), b)
                rows = new
            for g in range(16):
                at = g * 256 + half * 128
                out_ref[block, :, at : at + 128] = rows[g].astype(BF)


def regroup(pieces, order):
    return pl.pallas_call(
        regroup_kernel,
        out_shape=jax.ShapeDtypeStruct((2, 64, 4096), BF),
        in_specs=[pl.BlockSpec(memory_space=pltpu.SMEM), pl.BlockSpec(memory_space=pltpu.VMEM)],
        out_specs=pl.BlockSpec(memory_space=pltpu.VMEM),
        compiler_params=pltpu.CompilerParams(vmem_limit_bytes=40 << 20),
        cost_estimate=pl.CostEstimate(flops=2 * 10**9, bytes_accessed=0, transcendentals=0),
        name="regroup",
    )(order, pieces)


def bin_mask():
    row = lax.broadcasted_iota(jnp.int32, (8, 256), 0)
    lane = lax.broadcasted_iota(jnp.int32, (8, 256), 1)
    return (lane % 8 == row)[None]


def cross_bins(left, tiles, mask):
    left = jnp.where(mask, jnp.broadcast_to(left.astype(F32)[:, None, :], (64, 8, 256)), 0.0)
    left = left.astype(BF).reshape(512, 256)
    swapped = []
    for tile in tiles:
        wide = tile.astype(F32)
        swapped.append(jnp.concatenate([wide[8:16], -wide[0:8]], axis=0).astype(BF))
    right = jnp.concatenate([jnp.concatenate(tiles, axis=0), jnp.concatenate(swapped, axis=0)], axis=1)
    return jnp.dot(left, right, preferred_element_type=F32).reshape(64, 8, 256)


def store_bins(x_ref, at, first, second):
    both = jnp.concatenate([first, second], axis=1).astype(BF).reshape(64 // GROUP, GROUP, 16, 256)
    for q in range(2):
        for i in range(GROUP):
            x_ref[q, :, pl.ds(at, 16), 128 * i : 128 * i + 128] = both[:, i, :, 128 * q : 128 * q + 128]


def lags_kernel(held, fresh, place_ref, cos_ref, sin_ref, *refs):
    refs = list(refs)
    lefts = [refs.pop(0) for _ in range(fresh)]
    rights = [refs.pop(0) for _ in range(8)]
    xs = [refs.pop(0) for _ in range(held)]
    out_ref, x_ref, left_ref, right_ref, result_ref, x_sems, left_sems, right_sems, out_sems = refs

    def load_x(n):
        return pltpu.make_async_copy(xs[n], x_ref.at[n], x_sems.at[n])

    def load_left(n):
        return pltpu.make_async_copy(lefts[n], left_ref.at[n], left_sems.at[n])

    def load_right(n, a):
        return pltpu.make_async_copy(
            rights[a].at[place_ref[6 + held + n]], right_ref.at[n, a], right_sems.at[n, a]
        )

    for n in range(fresh):
        load_left(n).start()
        for a in range(8):
            load_right(n, a).start()
    for n in range(held):
        load_x(n).start()
    mask = bin_mask()
    def quarter(index, carry):
        n, part = index // 4, index % 4
        block, first = part // 2, 8 * (part % 2)

        @pl.when(part == 0)
        def arrived():
            pltpu.make_async_copy(lefts[0], left_ref.at[n], left_sems.at[n]).wait()
            for a in range(8):
                pltpu.make_async_copy(rights[a].at[0], right_ref.at[n, a], right_sems.at[n, a]).wait()

        def one(g):
            at = pl.multiple_of(g * 256, 256)
            tiles = [right_ref[n, a, w, block, g] for a in range(8) for w in range(2)]
            return cross_bins(left_ref[n, block, :, pl.ds(at, 256)], tiles, mask)

        for h in range(4):
            at = pl.multiple_of(part * 64 + 16 * h, 16)
            store_bins(x_ref.at[held + n], at, one(first + 2 * h), one(first + 2 * h + 1))
        return carry

    lax.fori_loop(0, 4 * fresh, quarter, 0)
    for n in range(held):
        load_x(n).wait()

    width = 128 * GROUP
    lane = lax.broadcasted_iota(jnp.int32, (1, width), 1)
    top = lax.broadcasted_iota(jnp.int32, (256, width), 0) == 0
    column = lax.broadcasted_iota(jnp.int32, (128, 128), 1)
    mirror = (128 - column) % 128

    def send(s, slot):
        return pltpu.make_async_copy(
            result_ref.at[slot], out_ref.at[pl.ds(s * STEP_I, STEP_I)], out_sems.at[slot]
        )

    def step(s, carry):
        slot = lax.rem(s, 2)

        @pl.when(s >= 2)
        def free():
            send(s - 2, slot).wait()

        for u in range(STEP_I // GROUP):
            at = s * (STEP_I // GROUP) + u
            even = odd = None
            for n in range(4):
                part = jnp.dot(cos_ref[place_ref[n]], x_ref[n, 0, at], preferred_element_type=F32)
                even = part if even is None else even + part
            for n in range(4):
                part = jnp.dot(sin_ref[place_ref[n]], x_ref[n, 1, at], preferred_element_type=F32)
                odd = part if odd is None else odd + part
            row_global = place_ref[4] * 64 + at * GROUP + lane // 128
            col_global = place_ref[5] * 128 + lane % 128
            factor = jnp.where(row_global == col_global, 0.0, 1.0 / math.sqrt(W * F)).astype(F32)
            even = even * factor
            odd = odd * factor
            later = even[0:256] - jnp.where(top, 0.0, odd)
            earlier = jnp.where(top, even[256:257], even[0:256]) + odd
            for i in range(GROUP):
                cols = slice(128 * i, 128 * i + 128)
                near = jnp.take_along_axis(earlier[0:128, cols].T, mirror, axis=1, mode="promise_in_bounds")
                away = jnp.take_along_axis(earlier[128:256, cols].T, mirror, axis=1, mode="promise_in_bounds")
                here = GROUP * u + i
                result_ref[slot, here, :, 0:128] = jnp.where(column == 0, near, away).astype(BF)
                result_ref[slot, here, :, 128:256] = jnp.where(column == 0, away, near).astype(BF)
                result_ref[slot, here, :, 256:512] = later[:, cols].T.astype(BF)
        send(s, slot).start()
        return carry

    steps = 64 // STEP_I
    lax.fori_loop(0, steps, step, 0)
    for s in range(steps - 2, steps):
        send(s, s % 2).wait()


def lags(place, lefts, rights, xs, tabs):
    cos, sin = tabs
    held, fresh = len(xs), len(lefts)
    whole = pl.BlockSpec(memory_space=pltpu.VMEM)
    remote = pl.BlockSpec(memory_space=pl.ANY)
    return pl.pallas_call(
        functools.partial(lags_kernel, held, fresh),
        out_shape=jax.ShapeDtypeStruct((64, 128, L), BF),
        in_specs=[pl.BlockSpec(memory_space=pltpu.SMEM), whole, whole] + [remote] * (fresh + 8 + held),
        out_specs=remote,
        scratch_shapes=[
            pltpu.VMEM((4, 2, 64 // GROUP, 256, 128 * GROUP), BF),
            pltpu.VMEM((fresh, 2, 64, 4096), BF),
            pltpu.VMEM((fresh, 8, 2, 2, 16, 16, 128), BF),
            pltpu.VMEM((2, STEP_I, 128, L), BF),
            pltpu.SemaphoreType.DMA((max(held, 1),)),
            pltpu.SemaphoreType.DMA((fresh,)),
            pltpu.SemaphoreType.DMA((fresh, 8)),
            pltpu.SemaphoreType.DMA((2,)),
        ],
        compiler_params=pltpu.CompilerParams(vmem_limit_bytes=60 << 20),
        cost_estimate=pl.CostEstimate(flops=18_000_000_000, bytes_accessed=36 * 2**20, transcendentals=0),
        name="lags",
    )(place, cos, sin, *lefts, *rights, *xs)


def marker_kernel(*refs):
    refs[-1][...] = jnp.zeros((8, 128), F32)


def marker(*after):
    return pl.pallas_call(
        marker_kernel,
        out_shape=jax.ShapeDtypeStruct((8, 128), F32),
        in_specs=[pl.BlockSpec(memory_space=pl.ANY)] * len(after),
        out_specs=pl.BlockSpec(memory_space=pltpu.VMEM),
        cost_estimate=pl.CostEstimate(flops=100_000_000_000, bytes_accessed=0, transcendentals=0),
        name="marker",
    )(*after)


def body(spectra):
    row = lax.axis_index("row")
    col = lax.axis_index("col")
    z, core = row // 4, row % 2
    y = col % 4
    near = jnp.where(core == 0, 3, 1)
    far = 4 - near
    place = jnp.stack(
        [y, (y + near) % 4, (y + far) % 4, (y + 2) % 4, row, col, 0 * y, 1 + core, 2 - core, 3 + 0 * y]
    ).astype(jnp.int32)
    blocks = jnp.stack([y, (y + 3) % 4, (y + 1) % 4, (y + 2) % 4]).astype(jnp.int32)

    both = ("row", "col")
    x = spectra.reshape(1024, 256)
    raw, first, last = turn(x)
    raw = lax.all_to_all(
        raw, ("row", "col"), split_axis=0, concat_axis=0, tiled=True, axis_index_groups=GROUPS_R
    )
    before = lax.ppermute(last, "col", [(i, i + 1) for i in range(COLS - 1)])
    after = lax.ppermute(first, "col", [(i + 1, i) for i in range(COLS - 1)])
    white = whiten_left(x, before, after)
    left = lax.all_to_all(
        white, ("row", "col"), split_axis=0, concat_axis=0, tiled=True, axis_index_groups=GROUPS_L
    )
    right = whiten_right(raw.reshape(2, 128, 16, 128), blocks, white)

    shift = jnp.stack([0 * z, 0 * z, near, near, 2 + 0 * z, far, far, 2 + 0 * z])
    swap = jnp.array([0, 1, 0, 1, 0, 1, 0, 1], jnp.int32)
    order = (((z + shift) % 4) * 4 + (core + swap) % 2)[:, None] + jnp.array([[0, 2]], jnp.int32)
    wait = lax.optimization_barrier
    right_later, left = wait((right, left))
    near_a = lax.ppermute(right_later, "row", Z_APART)
    sibling = lax.ppermute(right_later, "row", SIBLING)
    left = regroup(left, order.reshape(16).astype(jnp.int32))
    left_near = lax.ppermute(left, both, Y_APART)
    left_other = lax.ppermute(left, both, Y_AGAINST)
    near_b = lax.ppermute(sibling, "row", Z_APART)
    token = marker(left, sibling)

    left_near, near_a, token = wait((left_near, near_a, token))
    left_far = lax.ppermute(left_near, both, Y_APART)
    far_a = lax.ppermute(near_a, "row", Z_APART)
    token = marker(token)

    left_other, near_b, token = wait((left_other, near_b, token))
    swapped = [lax.ppermute(a, "row", SIBLING) for a in (near_a, near_b)]
    token = marker(token)
    left_far, far_a, token = wait((left_far, far_a, token))
    swapped.append(lax.ppermute(far_a, "row", SIBLING))
    token = marker(token)
    place, _ = wait((place, token))
    rights = [right, sibling, near_a, near_b, far_a] + swapped
    return lags(place, [left, left_near, left_other, left_far], rights, [], tables())


def solution(mesh):
    return jax.shard_map(
        body,
        mesh=mesh,
        in_specs=(P("row", None, None, "col"),),
        out_specs=P("row", "col", None),
        check_vma=False,
    )
```

```python
import functools
import math

import jax
import jax.numpy as jnp
import numpy as np
from jax import lax
from jax.experimental import pallas as pl
from jax.experimental.pallas import tpu as pltpu
from jax.sharding import PartitionSpec as P

F = 1024
L = 512
K = 8
W = 16
BF = jnp.bfloat16
F32 = jnp.float32

ROWS, COLS = 16, 8
SIBLING = [(r, r ^ 1) for r in range(16)]
Z_APART = [(r, (r + (4 if r % 2 == 0 else -4)) % 16) for r in range(16)]
Y_APART = [
    (r * 8 + c, r * 8 + ((c & 4) | ((c + (1 if r % 2 == 0 else -1)) & 3))) for r in range(16) for c in range(8)
]
Y_AGAINST = [(there, here) for here, there in Y_APART]
GROUPS_R = [
    [(z * 4 + xh * 2 + k) * 8 + c for xh in range(2) for c in range(8)]
    for z in range(4)
    for k in range(2)
]
GROUPS_L = [[r * 8 + xl * 4 + y for xl in range(2) for r in range(16)] for y in range(4)]
GROUP = 2
STEP_I = 16


def tables():
    freqs = np.arange(F)
    t_cos = np.concatenate([np.arange(257), np.zeros(15, np.int64)])
    t_sin = np.arange(256)
    t_sin[0] = 256
    cos = np.cos((t_cos[:, None] * freqs % (2 * F)) * (math.pi / F))
    sin = np.sin((t_sin[:, None] * freqs % (2 * F)) * (math.pi / F))
    cos[257:] = 0.0

    def by_block(table):
        blocks = table.reshape(table.shape[0], 2, 4, 128)
        return blocks.transpose(2, 0, 1, 3).reshape(4, table.shape[0], 256)

    return [jnp.asarray(a, BF) for a in (by_block(cos), by_block(sin))]


def band(copies):
    row = lax.broadcasted_iota(jnp.int32, (128, 144 * copies), 0)
    tap = lax.broadcasted_iota(jnp.int32, (128, 144 * copies), 1) % 144
    return jnp.where((tap >= row) & (tap <= row + 2 * K), 1.0, 0.0).astype(F32)


def turn_kernel(x_ref, right_ref, first_ref, last_ref):
    re = x_ref[:, 0:128].astype(F32).T
    im = x_ref[:, 128:256].astype(F32).T
    for g in range(16):
        both = jnp.concatenate([re[8 * g : 8 * g + 8], im[8 * g : 8 * g + 8]], axis=0).astype(BF)
        for c in range(COLS):
            right_ref[c, g] = both[:, 128 * c : 128 * c + 128]
            right_ref[COLS + c, g] = both[:, 128 * c : 128 * c + 128]
        if g == 0:
            first_ref[...] = both
        if g == 15:
            last_ref[...] = both


def turn(x):
    return pl.pallas_call(
        turn_kernel,
        out_shape=(
            jax.ShapeDtypeStruct((2 * COLS, 16, 16, 128), BF),
            jax.ShapeDtypeStruct((16, 1024), BF),
            jax.ShapeDtypeStruct((16, 1024), BF),
        ),
        compiler_params=pltpu.CompilerParams(vmem_limit_bytes=40 << 20),
        name="turn",
    )(x)


def magnitude(a, b):
    return jnp.sqrt(a * a + b * b)


def whiten_left_kernel(x_ref, before_ref, after_ref, left_ref):
    re = x_ref[:, 0:128].astype(F32).T
    im = x_ref[:, 128:256].astype(F32).T
    before = before_ref[...].astype(F32)
    after = after_ref[...].astype(F32)
    extended = jnp.concatenate(
        [magnitude(before[0:8], before[8:16]), magnitude(re, im), magnitude(after[0:8], after[8:16])], axis=0
    )
    total = jnp.dot(band(1), extended, precision=lax.Precision.HIGHEST, preferred_element_type=F32)
    smooth = jnp.maximum(total / (2 * K + 1), 0.5)
    re = (re / smooth).T.astype(BF)
    im = (im / smooth).T.astype(BF)
    for copy in range(2):
        for r in range(ROWS):
            left_ref[copy * ROWS + r, :, 0:128] = re[64 * r : 64 * r + 64]
            left_ref[copy * ROWS + r, :, 128:256] = im[64 * r : 64 * r + 64]


def whiten_left(x, before, after):
    return pl.pallas_call(
        whiten_left_kernel,
        out_shape=jax.ShapeDtypeStruct((2 * ROWS, 64, 256), BF),
        compiler_params=pltpu.CompilerParams(vmem_limit_bytes=40 << 20),
        name="whiten_left",
    )(x, before, after)


def whiten_right_kernel(place_ref, x_ref, after_ref, out_ref, re_ref, im_ref, ext_ref):
    del after_ref
    re_ref[...] = x_ref[:, :, 0:8].astype(F32)
    im_ref[...] = x_ref[:, :, 8:16].astype(F32)
    for w in range(2):
        ext_ref[0:8, 128 * w : 128 * w + 128] = jnp.zeros((8, 128), F32)
        ext_ref[1032:1040, 128 * w : 128 * w + 128] = jnp.zeros((8, 128), F32)
        ext_ref[8:1032, 128 * w : 128 * w + 128] = magnitude(re_ref[w], im_ref[w]).reshape(1024, 128)
    bands = band(3).astype(BF)
    for block in range(8):
        wide = ext_ref[128 * block : 128 * block + 144]
        high = wide.astype(BF)
        rest = wide - high.astype(F32)
        middle = rest.astype(BF)
        low = (rest - middle.astype(F32)).astype(BF)
        total = jnp.dot(
            bands, jnp.concatenate([high, middle, low], axis=0), preferred_element_type=F32
        )
        smooth = jnp.maximum(total / (2 * K + 1), 0.5)
        for w in range(2):
            here = smooth[:, 128 * w : 128 * w + 128].reshape(16, 8, 128)
            rows = slice(16 * block, 16 * block + 16)
            re_ref[w, rows] = re_ref[w, rows] / here
            im_ref[w, rows] = im_ref[w, rows] / here
    for n in range(4):
        for half in range(2):
            rows = pl.ds((place_ref[n] + 4 * half) * 16, 16)
            for w in range(2):
                both = jnp.concatenate([re_ref[w, rows], im_ref[w, rows]], axis=1).astype(BF)
                out_ref[n, w, half] = both


def whiten_right(raw, place, after):
    return pl.pallas_call(
        whiten_right_kernel,
        out_shape=jax.ShapeDtypeStruct((4, 2, 2, 16, 16, 128), BF),
        in_specs=[
            pl.BlockSpec(memory_space=pltpu.SMEM),
            pl.BlockSpec(memory_space=pltpu.VMEM),
            pl.BlockSpec(memory_space=pl.ANY),
        ],
        out_specs=pl.BlockSpec(memory_space=pltpu.VMEM),
        scratch_shapes=[
            pltpu.VMEM((2, 128, 8, 128), F32),
            pltpu.VMEM((2, 128, 8, 128), F32),
            pltpu.VMEM((1040, 256), F32),
        ],
        compiler_params=pltpu.CompilerParams(vmem_limit_bytes=40 << 20),
        name="whiten_right",
    )(place, raw, after)


def regroup_kernel(order_ref, in_ref, out_ref):
    granule = lax.broadcasted_iota(jnp.int32, (64, 128), 1) // 8
    for block in range(2):
        for half in range(2):
            rows = []
            for slot in range(8):
                window = order_ref[half * 8 + slot]
                for p in range(2):
                    rows.append(in_ref[block * 16 + window, :, 128 * p : 128 * p + 128].astype(F32))
            for bit in (1, 2, 4, 8):
                low = (granule & bit) == 0
                new = list(rows)
                for u in range(16):
                    if u & bit:
                        continue
                    a, b = rows[u], rows[u | bit]
                    new[u] = jnp.where(low, a, pltpu.roll(b, 8 * bit, 1))
                    new[u | bit] = jnp.where(low, pltpu.roll(a, 128 - 8 * bit, 1), b)
                rows = new
            for g in range(16):
                at = g * 256 + half * 128
                out_ref[block, :, at : at + 128] = rows[g].astype(BF)


def regroup(pieces, order):
    return pl.pallas_call(
        regroup_kernel,
        out_shape=jax.ShapeDtypeStruct((2, 64, 4096), BF),
        in_specs=[pl.BlockSpec(memory_space=pltpu.SMEM), pl.BlockSpec(memory_space=pltpu.VMEM)],
        out_specs=pl.BlockSpec(memory_space=pltpu.VMEM),
        compiler_params=pltpu.CompilerParams(vmem_limit_bytes=40 << 20),
        cost_estimate=pl.CostEstimate(flops=2 * 10**9, bytes_accessed=0, transcendentals=0),
        name="regroup",
    )(order, pieces)


def bin_mask():
    row = lax.broadcasted_iota(jnp.int32, (8, 256), 0)
    lane = lax.broadcasted_iota(jnp.int32, (8, 256), 1)
    return (lane % 8 == row)[None]


def cross_bins(left, tiles, mask):
    left = jnp.where(mask, jnp.broadcast_to(left.astype(F32)[:, None, :], (64, 8, 256)), 0.0)
    left = left.astype(BF).reshape(512, 256)
    swapped = []
    for tile in tiles:
        wide = tile.astype(F32)
        swapped.append(jnp.concatenate([wide[8:16], -wide[0:8]], axis=0).astype(BF))
    right = jnp.concatenate([jnp.concatenate(tiles, axis=0), jnp.concatenate(swapped, axis=0)], axis=1)
    return jnp.dot(left, right, preferred_element_type=F32).reshape(64, 8, 256)


def store_bins(x_ref, at, first, second):
    both = jnp.concatenate([first, second], axis=1).astype(BF).reshape(64 // GROUP, GROUP, 16, 256)
    for q in range(2):
        for i in range(GROUP):
            x_ref[q, :, pl.ds(at, 16), 128 * i : 128 * i + 128] = both[:, i, :, 128 * q : 128 * q + 128]


def lags_kernel(held, fresh, place_ref, cos_ref, sin_ref, *refs):
    refs = list(refs)
    lefts = [refs.pop(0) for _ in range(fresh)]
    rights = [refs.pop(0) for _ in range(8)]
    xs = [refs.pop(0) for _ in range(held)]
    out_ref, x_ref, left_ref, right_ref, result_ref, x_sems, left_sems, right_sems, out_sems = refs

    def load_x(n):
        return pltpu.make_async_copy(xs[n], x_ref.at[n], x_sems.at[n])

    def load_left(n):
        return pltpu.make_async_copy(lefts[n], left_ref.at[n], left_sems.at[n])

    def load_right(n, a):
        return pltpu.make_async_copy(
            rights[a].at[place_ref[6 + held + n]], right_ref.at[n, a], right_sems.at[n, a]
        )

    for n in range(fresh):
        load_left(n).start()
        for a in range(8):
            load_right(n, a).start()
    for n in range(held):
        load_x(n).start()
    mask = bin_mask()
    def quarter(index, carry):
        n, part = index // 4, index % 4
        block, first = part // 2, 8 * (part % 2)

        @pl.when(part == 0)
        def arrived():
            pltpu.make_async_copy(lefts[0], left_ref.at[n], left_sems.at[n]).wait()
            for a in range(8):
                pltpu.make_async_copy(rights[a].at[0], right_ref.at[n, a], right_sems.at[n, a]).wait()

        def one(g):
            at = pl.multiple_of(g * 256, 256)
            tiles = [right_ref[n, a, w, block, g] for a in range(8) for w in range(2)]
            return cross_bins(left_ref[n, block, :, pl.ds(at, 256)], tiles, mask)

        for h in range(4):
            at = pl.multiple_of(part * 64 + 16 * h, 16)
            store_bins(x_ref.at[held + n], at, one(first + 2 * h), one(first + 2 * h + 1))
        return carry

    lax.fori_loop(0, 4 * fresh, quarter, 0)
    for n in range(held):
        load_x(n).wait()

    width = 128 * GROUP
    lane = lax.broadcasted_iota(jnp.int32, (1, width), 1)
    top = lax.broadcasted_iota(jnp.int32, (256, width), 0) == 0
    column = lax.broadcasted_iota(jnp.int32, (128, 128), 1)
    mirror = (128 - column) % 128

    def send(s, slot):
        return pltpu.make_async_copy(
            result_ref.at[slot], out_ref.at[pl.ds(s * STEP_I, STEP_I)], out_sems.at[slot]
        )

    def step(s, carry):
        slot = lax.rem(s, 2)

        @pl.when(s >= 2)
        def free():
            send(s - 2, slot).wait()

        for u in range(STEP_I // GROUP):
            at = s * (STEP_I // GROUP) + u
            even = odd = None
            for n in range(4):
                part = jnp.dot(cos_ref[place_ref[n]], x_ref[n, 0, at], preferred_element_type=F32)
                even = part if even is None else even + part
            for n in range(4):
                part = jnp.dot(sin_ref[place_ref[n]], x_ref[n, 1, at], preferred_element_type=F32)
                odd = part if odd is None else odd + part
            row_global = place_ref[4] * 64 + at * GROUP + lane // 128
            col_global = place_ref[5] * 128 + lane % 128
            factor = jnp.where(row_global == col_global, 0.0, 1.0 / math.sqrt(W * F)).astype(F32)
            even = even * factor
            odd = odd * factor
            later = even[0:256] - jnp.where(top, 0.0, odd)
            earlier = jnp.where(top, even[256:257], even[0:256]) + odd
            for i in range(GROUP):
                cols = slice(128 * i, 128 * i + 128)
                near = jnp.take_along_axis(earlier[0:128, cols].T, mirror, axis=1, mode="promise_in_bounds")
                away = jnp.take_along_axis(earlier[128:256, cols].T, mirror, axis=1, mode="promise_in_bounds")
                here = GROUP * u + i
                result_ref[slot, here, :, 0:128] = jnp.where(column == 0, near, away).astype(BF)
                result_ref[slot, here, :, 128:256] = jnp.where(column == 0, away, near).astype(BF)
                result_ref[slot, here, :, 256:512] = later[:, cols].T.astype(BF)
        send(s, slot).start()
        return carry

    steps = 64 // STEP_I
    lax.fori_loop(0, steps, step, 0)
    for s in range(steps - 2, steps):
        send(s, s % 2).wait()


def lags(place, lefts, rights, xs, tabs):
    cos, sin = tabs
    held, fresh = len(xs), len(lefts)
    whole = pl.BlockSpec(memory_space=pltpu.VMEM)
    remote = pl.BlockSpec(memory_space=pl.ANY)
    return pl.pallas_call(
        functools.partial(lags_kernel, held, fresh),
        out_shape=jax.ShapeDtypeStruct((64, 128, L), BF),
        in_specs=[pl.BlockSpec(memory_space=pltpu.SMEM), whole, whole] + [remote] * (fresh + 8 + held),
        out_specs=remote,
        scratch_shapes=[
            pltpu.VMEM((4, 2, 64 // GROUP, 256, 128 * GROUP), BF),
            pltpu.VMEM((fresh, 2, 64, 4096), BF),
            pltpu.VMEM((fresh, 8, 2, 2, 16, 16, 128), BF),
            pltpu.VMEM((2, STEP_I, 128, L), BF),
            pltpu.SemaphoreType.DMA((max(held, 1),)),
            pltpu.SemaphoreType.DMA((fresh,)),
            pltpu.SemaphoreType.DMA((fresh, 8)),
            pltpu.SemaphoreType.DMA((2,)),
        ],
        compiler_params=pltpu.CompilerParams(vmem_limit_bytes=60 << 20),
        cost_estimate=pl.CostEstimate(flops=18_000_000_000, bytes_accessed=36 * 2**20, transcendentals=0),
        name="lags",
    )(place, cos, sin, *lefts, *rights, *xs)


def marker_kernel(*refs):
    refs[-1][...] = jnp.zeros((8, 128), F32)


def marker(*after):
    return pl.pallas_call(
        marker_kernel,
        out_shape=jax.ShapeDtypeStruct((8, 128), F32),
        in_specs=[pl.BlockSpec(memory_space=pl.ANY)] * len(after),
        out_specs=pl.BlockSpec(memory_space=pltpu.VMEM),
        cost_estimate=pl.CostEstimate(flops=100_000_000_000, bytes_accessed=0, transcendentals=0),
        name="marker",
    )(*after)


def body(spectra):
    row = lax.axis_index("row")
    col = lax.axis_index("col")
    z, core = row // 4, row % 2
    y = col % 4
    near = jnp.where(core == 0, 3, 1)
    far = 4 - near
    place = jnp.stack(
        [y, (y + near) % 4, (y + far) % 4, (y + 2) % 4, row, col, 0 * y, 1 + core, 2 - core, 3 + 0 * y]
    ).astype(jnp.int32)
    blocks = jnp.stack([y, (y + 3) % 4, (y + 1) % 4, (y + 2) % 4]).astype(jnp.int32)

    both = ("row", "col")
    x = spectra.reshape(1024, 256)
    raw, first, last = turn(x)
    raw = lax.all_to_all(
        raw, ("row", "col"), split_axis=0, concat_axis=0, tiled=True, axis_index_groups=GROUPS_R
    )
    before = lax.ppermute(last, "col", [(i, i + 1) for i in range(COLS - 1)])
    after = lax.ppermute(first, "col", [(i + 1, i) for i in range(COLS - 1)])
    white = whiten_left(x, before, after)
    left = lax.all_to_all(
        white, ("row", "col"), split_axis=0, concat_axis=0, tiled=True, axis_index_groups=GROUPS_L
    )
    right = whiten_right(raw.reshape(2, 128, 16, 128), blocks, white)

    shift = jnp.stack([0 * z, 0 * z, near, near, 2 + 0 * z, far, far, 2 + 0 * z])
    swap = jnp.array([0, 1, 0, 1, 0, 1, 0, 1], jnp.int32)
    order = (((z + shift) % 4) * 4 + (core + swap) % 2)[:, None] + jnp.array([[0, 2]], jnp.int32)
    wait = lax.optimization_barrier
    sibling = lax.ppermute(right, "row", SIBLING)
    right_later, sibling, left = wait((right, sibling, left))
    near_a = lax.ppermute(right_later, "row", Z_APART)
    left = regroup(left, order.reshape(16).astype(jnp.int32))
    left_near = lax.ppermute(left, both, Y_APART)
    left_other = lax.ppermute(left, both, Y_AGAINST)
    near_b = lax.ppermute(sibling, "row", Z_APART)
    token = marker(left, sibling)

    left_near, near_a, token = wait((left_near, near_a, token))
    left_far = lax.ppermute(left_near, both, Y_APART)
    far_a = lax.ppermute(near_a, "row", Z_APART)
    token = marker(token)

    left_other, near_b, token = wait((left_other, near_b, token))
    swapped = [lax.ppermute(a, "row", SIBLING) for a in (near_a, near_b)]
    token = marker(token)
    left_far, far_a, token = wait((left_far, far_a, token))
    swapped.append(lax.ppermute(far_a, "row", SIBLING))
    token = marker(token)
    place, _ = wait((place, token))
    rights = [right, sibling, near_a, near_b, far_a] + swapped
    return lags(place, [left, left_near, left_other, left_far], rights, [], tables())


def solution(mesh):
    return jax.shard_map(
        body,
        mesh=mesh,
        in_specs=(P("row", None, None, "col"),),
        out_specs=P("row", "col", None),
        check_vma=False,
    )
```
